32 devices in a mesh: dp: 8 (over z, core), tensor: 4 (over y, x).
Axes of the slice: x: 2, y: 2, z: 4, core: 2. Of those that a mesh axis runs over, the one named last changes fastest.
Arguments:
- acts: bfloat16 [1024, 8192], P('dp', 'tensor'), may hold values from -6 to 6
- grad_out: bfloat16 [1024, 14336], P('dp', 'tensor'), may hold values from -6 to 6
- proj_t: bfloat16 [512, 8192], P(None, 'tensor'), may hold values from -6 to 6
- first_moment: float32 [512, 14336], P('dp', 'tensor'), may hold values from -0.15625 to 0.15625
- second_moment: float32 [512, 14336], P('dp', 'tensor'), may hold values from 1e-05 to 0.001
Outputs:
- adam_step: float32 [512, 14336], P('dp', 'tensor')
- new_proj_t: float32 [512, 8192], P('dp', 'tensor')
The draws below stay inside these ranges and needn't reach their ends.
All inputs are finite; a program needn't handle non-finite values.
Results may differ from the reference program's by a relative error of at most 0.023.
Values may be sent and summed in bfloat16 or wider, within the bound.
A program may use at most 64 MiB of HBM per device.

```python
import math
import jax
import jax.numpy as jnp
from jax import lax

D = 8192
F = 14336
R = 512
TOKENS = 1024
N_TENSOR = 4


def block_levels(stream_key, dims, shards, least, high):
    loudness, own = 1.0, jax.random.fold_in(stream_key, 6)
    for position, parts in shards:
        draws = jnp.exp(jax.random.uniform(jax.random.fold_in(own, position), (parts,), jnp.float32, least / len(shards), high / len(shards)))
        loudness = loudness * jnp.repeat(draws, dims[position] // parts).reshape([-1 if axis == position else 1 for axis in range(len(dims))])
    return loudness


def bell_draw(key, shape, deviation, bound, pieces=(), held_as=jnp.bfloat16):
    entries = jax.random.normal(key, shape, jnp.float32) * deviation
    if len(pieces) > 0:
        entries = block_levels(key, shape, pieces, -0.22, 0.18) * entries
    return jnp.clip(entries, min=-bound, max=bound).astype(held_as)


def setup_inputs(seed: int = 0) -> dict:
    arg_keys = jax.random.split(jax.random.key(seed), 6)
    return {
        "acts": bell_draw(arg_keys[0], (TOKENS, D), 1.0, 6.0, ((0, 8), (1, 4))),
        "grad_out": bell_draw(arg_keys[1], (TOKENS, F), 1.0, 6.0, ((0, 8), (1, 4))),
        "proj_t": bell_draw(arg_keys[2], (R, D), 1.0, 6.0, ((1, 4),)),
        "first_moment": bell_draw(arg_keys[3], (R, F), 0.01, 0.15625, ((0, 8), (1, 4)), jnp.float32),
        "second_moment": jnp.clip(jnp.exp(math.log(0.001) - 4.6051703 * jax.random.uniform(arg_keys[4], (R, F), jnp.float32) ** block_levels(arg_keys[4], (R, F), ((0, 8), (1, 4)), -0.2, 0.2)), 9.999999747378752e-06, 0.001),
    }


def rounded_sum(terms):
    total = jnp.zeros(terms[0].shape, jnp.float32)
    for term in terms:
        low_term = lax.optimization_barrier(term.astype(jnp.bfloat16))
        total = total + low_term.astype(jnp.float32)
    return total

def reference(acts, grad_out, proj_t, first_moment, second_moment):
    inv_root = 1.0 / jnp.sqrt(jnp.float32(D))
    width_blk = D // N_TENSOR
    hidden_blk = F // N_TENSOR
    coord_terms = []
    for block in range(N_TENSOR):
        lo = block * width_blk
        part = lax.dot_general(acts[:, lo:lo + width_blk], proj_t[:, lo:lo + width_blk], (((1,), (1,)), ((), ())), preferred_element_type=jnp.float32)
        coord_terms.append(part * inv_root)
    coords = rounded_sum(coord_terms).astype(jnp.bfloat16)
    proj_grad = lax.dot_general(coords, grad_out, (((0,), (0,)), ((), ())), preferred_element_type=jnp.float32) / TOKENS
    moment_one = 0.9 * first_moment + 0.1 * proj_grad
    moment_two = 0.999 * second_moment + 0.001 * proj_grad * proj_grad
    adam_step = moment_one / (1.0 - 0.9 ** 10) / (jnp.sqrt(moment_two / (1.0 - 0.999 ** 10)) + 1e-08)
    low = proj_grad.astype(jnp.bfloat16)
    back_terms = []
    cross_terms = []
    for block in range(N_TENSOR):
        lo = block * hidden_blk
        low_blk = low[:, lo:lo + hidden_blk]
        back_terms.append(lax.dot_general(grad_out[:, lo:lo + hidden_blk], low_blk, (((1,), (1,)), ((), ())), preferred_element_type=jnp.float32))
        cross_terms.append(lax.dot_general(low_blk, low_blk, (((1,), (1,)), ((), ())), preferred_element_type=jnp.float32))
    back = rounded_sum(back_terms)
    cross = rounded_sum(cross_terms)
    back_low = back.astype(jnp.bfloat16)
    pull = lax.dot_general(back_low, acts, (((0,), (0,)), ((), ())), preferred_element_type=jnp.float32) / TOKENS
    proj_wide = proj_t.astype(jnp.float32)
    correction = jnp.dot(cross, proj_wide, precision=lax.Precision.HIGHEST)
    new_proj_t = proj_wide + jnp.sqrt(jnp.float32(D)) * pull - correction
    return (adam_step, new_proj_t)
```

```python
import functools

import jax
import jax.numpy as jnp
from jax import lax
from jax.experimental import pallas as pl
from jax.experimental.pallas import tpu as pltpu
from jax.sharding import PartitionSpec as P

MESH = pl.DeviceIdType.MESH
ANY = pl.BlockSpec(memory_space=pl.ANY)
VMEM = pl.BlockSpec(memory_space=pltpu.VMEM)


def contract_rows(left, right):
    return lax.dot_general(
        left, right, (((0,), (0,)), ((), ())), preferred_element_type=jnp.float32
    )


def contract_cols(left, right):
    return lax.dot_general(
        left, right, (((1,), (1,)), ((), ())), preferred_element_type=jnp.float32
    )


def place():
    dp = lax.axis_index("dp")
    return dp, lax.div(dp, 2), lax.rem(dp, 2), lax.axis_index("tensor")


def greet(n_dp, n_ten):
    dp, _, _, ten = place()
    barrier = pltpu.get_barrier_semaphore()
    for k in range(1, n_dp):
        pl.semaphore_signal(
            barrier, inc=1, device_id=(lax.rem(dp + k, n_dp), ten), device_id_type=MESH
        )
    for k in range(1, n_ten):
        pl.semaphore_signal(
            barrier, inc=1, device_id=(dp, lax.rem(ten + k, n_ten)), device_id_type=MESH
        )
    pl.semaphore_wait(barrier, n_dp + n_ten - 2)


def send(src, dst, sems, k, device):
    copy = pltpu.make_async_remote_copy(
        src_ref=src,
        dst_ref=dst,
        send_sem=sems.at[0, k],
        recv_sem=sems.at[1, k],
        device_id=device,
        device_id_type=MESH,
    )
    copy.start()
    return copy


def start_swap(src, dst, sems, n_dp):
    dp, _, _, ten = place()
    copies = []
    for k in range(1, n_dp):
        peer = lax.rem(dp + k, n_dp)
        copies.append(send(src.at[peer], dst.at[dp], sems, k, (peer, ten)))
    own = pltpu.make_async_copy(src.at[dp], dst.at[dp], sems.at[0, 0])
    own.start()
    return copies + [own]


def wait_all(copies):
    for copy in copies:
        copy.wait()


def reduce_stage(src, got, sems, me, n, device):
    copies = []
    for k in range(1, n):
        peer = lax.rem(me + k, n)
        copies.append(send(src.at[peer], got.at[k], sems, k, device(peer)))
    total = src[me].astype(jnp.float32)
    for k in range(1, n):
        copies[k - 1].wait()
        total = total + got[k].astype(jnp.float32)
    return total


def gather_stages(full, sems_z, sems_t, sems_c, n_z, n_ten):
    _, z, c, ten = place()
    copies = []
    mine = full.at[c, ten, z]
    for k in range(1, n_z):
        peer = lax.rem(z + k, n_z)
        copies.append(send(mine, mine, sems_z, k, (peer * 2 + c, ten)))
    wait_all(copies)
    copies = []
    mine = full.at[c, ten]
    for k in range(1, n_ten):
        peer = lax.rem(ten + k, n_ten)
        copies.append(send(mine, mine, sems_t, k, (z * 2 + c, peer)))
    wait_all(copies)
    mine = full.at[c]
    send(mine, mine, sems_c, 1, (z * 2 + 1 - c, ten)).wait()


def coords_kernel(n_dp, n_ten, g8, part, g_all, full_out, full, got, s_g, s_r, s_z, s_t, s_c):
    n_z = n_dp // 2
    dp, z, c, ten = place()
    greet(n_dp, n_ten)
    total = reduce_stage(part, got, s_r, ten, n_ten, lambda p: (dp, p))
    swaps = start_swap(g8, g_all, s_g, n_dp)
    full[c, ten, z] = total.astype(full.dtype)
    gather_stages(full, s_z, s_t, s_c, n_z, n_ten)
    out = pltpu.make_async_copy(full, full_out, s_c.at[0, 0])
    out.start()
    wait_all(swaps + [out])


def back_kernel(
    n_dp, n_ten, low8, a8, part, low_all, a_all, full_out,
    full, got_c, mid_c, got_t, mid_t, got_z, s_l, s_a, s_rc, s_rt, s_rz, s_z, s_t, s_c,
):
    n_z = n_dp // 2
    dp, z, c, ten = place()
    greet(n_dp, n_ten)
    mid_c[...] = reduce_stage(
        part, got_c, s_rc, c, 2, lambda p: (z * 2 + p, ten)
    ).astype(mid_c.dtype)
    swaps = start_swap(low8, low_all, s_l, n_dp) + start_swap(a8, a_all, s_a, n_dp)
    mid_t[...] = reduce_stage(
        mid_c, got_t, s_rt, ten, n_ten, lambda p: (dp, p)
    ).astype(mid_t.dtype)
    total = reduce_stage(mid_t, got_z, s_rz, z, n_z, lambda p: (p * 2 + c, ten))
    full[c, ten, z] = total.astype(full.dtype)
    gather_stages(full, s_z, s_t, s_c, n_z, n_ten)
    out = pltpu.make_async_copy(full, full_out, s_c.at[0, 0])
    out.start()
    wait_all(swaps + [out])


def swap_kernel(n_dp, src, dst, sems):
    greet(n_dp, 1)
    wait_all(start_swap(src, dst, sems, n_dp))


def pairs(n):
    return pltpu.SemaphoreType.DMA((2, n))


def params(which):
    return pltpu.CompilerParams(
        collective_id=which, has_side_effects=True, vmem_limit_bytes=32 * 2**20
    )


def like(shape, dtype=jnp.bfloat16):
    return jax.ShapeDtypeStruct(shape, dtype)


def to_blocks(x, n, width):
    rows, cols = x.shape
    x = x.reshape(rows, n, cols // n).transpose(1, 0, 2)
    return jnp.pad(x, ((0, 0), (0, 0), (0, width - cols // n)))


def direct(n_dp, n_ten, acts, grad_out, proj_t, first_moment, second_moment):
    n_z = n_dp // 2
    tok_rows, width = acts.shape
    hidden = grad_out.shape[1]
    rank = proj_t.shape[0]
    rank_rows = first_moment.shape[0]
    tokens = tok_rows * n_dp
    dim = jnp.float32(width * n_ten)
    bf16 = jnp.bfloat16
    h_blk = hidden // n_dp
    h_pad = -(-h_blk // 128) * 128
    w_blk = width // n_dp
    sub = tok_rows // n_ten

    part = (contract_cols(acts, proj_t) * (1.0 / jnp.sqrt(dim))).astype(bf16)
    g8 = to_blocks(grad_out, n_dp, h_pad)
    g_all, coords = pl.pallas_call(
        functools.partial(coords_kernel, n_dp, n_ten),
        out_shape=(like(g8.shape), like((2, n_ten, n_z, sub, rank))),
        in_specs=[ANY, VMEM],
        out_specs=(ANY, ANY),
        scratch_shapes=[
            pltpu.VMEM((2, n_ten, n_z, sub, rank), bf16),
            pltpu.VMEM((n_ten, sub, rank), bf16),
            pairs(n_dp), pairs(n_ten), pairs(n_z), pairs(n_ten), pairs(2),
        ],
        compiler_params=params(0),
    )(g8, part.reshape(n_ten, sub, rank))
    coords = coords.transpose(2, 0, 1, 3, 4).reshape(tokens, rank)
    g_all = g_all.reshape(tokens, h_pad)

    low = (contract_rows(coords, g_all) / tokens).astype(bf16)
    back_part = contract_cols(g_all, low).astype(bf16)
    cross_part = contract_cols(low, low).astype(bf16)
    both = tokens + rank
    blk = both // (n_dp * n_ten)
    joined = jnp.concatenate([back_part, cross_part], axis=0)
    joined = joined.reshape(2, n_ten, n_z, blk, rank)
    a8 = to_blocks(acts, n_dp, w_blk)
    low8 = low.reshape(n_dp, rank_rows, h_pad)
    low_all, a_all, sums = pl.pallas_call(
        functools.partial(back_kernel, n_dp, n_ten),
        out_shape=(like(low8.shape), like(a8.shape), like(joined.shape)),
        in_specs=[ANY, ANY, VMEM],
        out_specs=(ANY, ANY, ANY),
        scratch_shapes=[
            pltpu.VMEM(joined.shape, bf16),
            pltpu.VMEM(joined.shape, bf16),
            pltpu.VMEM(joined.shape[1:], bf16),
            pltpu.VMEM(joined.shape[1:], bf16),
            pltpu.VMEM(joined.shape[2:], bf16),
            pltpu.VMEM(joined.shape[2:], bf16),
            pairs(n_dp), pairs(n_dp), pairs(2), pairs(n_ten), pairs(n_z),
            pairs(n_z), pairs(n_ten), pairs(2),
        ],
        compiler_params=params(1),
    )(low8, a8, joined)
    sums = sums.reshape(both, rank)
    back_low, cross = sums[:tokens], sums[tokens:]

    dp = lax.axis_index("dp")
    pull = contract_rows(back_low, a_all.reshape(tokens, w_blk)) / tokens
    own_cols = lax.dynamic_slice_in_dim(proj_t, dp * w_blk, w_blk, 1)
    correction = jnp.dot(cross, own_cols, preferred_element_type=jnp.float32)
    delta = (jnp.sqrt(dim) * pull - correction).astype(bf16)
    d8 = delta.reshape(n_dp, rank_rows, w_blk)
    d_all = pl.pallas_call(
        functools.partial(swap_kernel, n_dp),
        out_shape=like(d8.shape),
        in_specs=[ANY],
        out_specs=ANY,
        scratch_shapes=[pairs(n_dp)],
        compiler_params=params(2),
    )(d8)
    own_rows = lax.dynamic_slice_in_dim(proj_t, dp * rank_rows, rank_rows, 0)
    step = d_all.transpose(1, 0, 2).reshape(rank_rows, width)
    new_proj_t = own_rows.astype(jnp.float32) + step.astype(jnp.float32)

    grad_part = low_all[:, :, :h_blk].transpose(1, 0, 2).reshape(rank_rows, hidden)
    return adam(grad_part.astype(jnp.float32), first_moment, second_moment), new_proj_t


def adam(grad_part, first_moment, second_moment):
    moment_one = 0.9 * first_moment + 0.1 * grad_part
    moment_two = 0.999 * second_moment + 0.001 * grad_part * grad_part
    return moment_one / (1.0 - 0.9**10) / (jnp.sqrt(moment_two / (1.0 - 0.999**10)) + 1e-08)


def general(acts, grad_out, proj_t, first_moment, second_moment):
    tok_rows, width = acts.shape
    dim = jnp.float32(width * lax.axis_size("tensor"))
    total_tokens = tok_rows * lax.axis_size("dp")
    rank_rows = first_moment.shape[0]
    row_start = lax.axis_index("dp") * rank_rows
    local_coords = contract_cols(acts, proj_t) * (1.0 / jnp.sqrt(dim))
    coords = lax.psum(local_coords.astype(jnp.bfloat16), "tensor")
    grad_part = lax.psum_scatter(
        contract_rows(coords, grad_out) / total_tokens, "dp", scatter_dimension=0, tiled=True
    )
    low_part = grad_part.astype(jnp.bfloat16)
    piece = lax.all_gather(low_part, "dp", axis=0, tiled=True)
    back = lax.psum(contract_cols(grad_out, piece).astype(jnp.bfloat16), "tensor")
    cross = lax.psum(contract_cols(low_part, piece).astype(jnp.bfloat16), "tensor")
    pull = lax.psum_scatter(
        contract_rows(back, acts) / total_tokens, "dp", scatter_dimension=0, tiled=True
    )
    own_rows = lax.dynamic_slice_in_dim(proj_t, row_start, rank_rows, 0)
    correction = jnp.dot(
        cross.astype(jnp.float32), proj_t.astype(jnp.float32), precision=lax.Precision.HIGHEST
    )
    new_proj_t = own_rows.astype(jnp.float32) + jnp.sqrt(dim) * pull - correction
    return adam(grad_part, first_moment, second_moment), new_proj_t


def local(n_dp, n_ten, acts, grad_out, proj_t, first_moment, second_moment):
    tok_rows, width = acts.shape
    both = tok_rows * n_dp + proj_t.shape[0]
    fits = (
        n_dp % 2 == 0
        and n_dp <= 16
        and tok_rows % (16 * n_ten) == 0
        and both % (16 * n_dp * n_ten) == 0
        and first_moment.shape[0] % 16 == 0
        and width % (128 * n_dp) == 0
        and grad_out.shape[1] % n_dp == 0
    )
    args = (acts, grad_out, proj_t, first_moment, second_moment)
    return direct(n_dp, n_ten, *args) if fits else general(*args)


def solution(mesh):
    split = P("dp", "tensor")
    return jax.shard_map(
        functools.partial(local, mesh.shape["dp"], mesh.shape["tensor"]),
        mesh=mesh,
        in_specs=(split, split, P(None, "tensor"), split, split),
        out_specs=(split, split),
        check_vma=False,
    )
```

```python
import functools

import jax
import jax.numpy as jnp
from jax import lax
from jax.experimental import pallas as pl
from jax.experimental.pallas import tpu as pltpu
from jax.sharding import PartitionSpec as P

MESH = pl.DeviceIdType.MESH
ANY = pl.BlockSpec(memory_space=pl.ANY)
VMEM = pl.BlockSpec(memory_space=pltpu.VMEM)
PARTS = 3


def contract_rows(left, right):
    return lax.dot_general(
        left, right, (((0,), (0,)), ((), ())), preferred_element_type=jnp.float32
    )


def contract_cols(left, right):
    return lax.dot_general(
        left, right, (((1,), (1,)), ((), ())), preferred_element_type=jnp.float32
    )


def place():
    dp = lax.axis_index("dp")
    return dp, lax.div(dp, 2), lax.rem(dp, 2), lax.axis_index("tensor")


def greet(n_dp, n_ten):
    dp, _, _, ten = place()
    barrier = pltpu.get_barrier_semaphore()
    for k in range(1, n_dp):
        pl.semaphore_signal(
            barrier, inc=1, device_id=(lax.rem(dp + k, n_dp), ten), device_id_type=MESH
        )
    for k in range(1, n_ten):
        pl.semaphore_signal(
            barrier, inc=1, device_id=(dp, lax.rem(ten + k, n_ten)), device_id_type=MESH
        )
    pl.semaphore_wait(barrier, n_dp + n_ten - 2)


def send(src, dst, sems, k, device):
    copy = pltpu.make_async_remote_copy(
        src_ref=src,
        dst_ref=dst,
        send_sem=sems.at[0, k],
        recv_sem=sems.at[1, k],
        device_id=device,
        device_id_type=MESH,
    )
    copy.start()
    return copy


def start_swap(src, dst, sems, n_dp, steps=None):
    dp, _, _, ten = place()
    copies = []
    for k in steps or range(1, n_dp):
        peer = lax.rem(dp + k, n_dp)
        copies.append(send(src.at[peer], dst.at[dp], sems, k, (peer, ten)))
    return copies


def start_own(src, dst, sems):
    dp = place()[0]
    own = pltpu.make_async_copy(src.at[dp], dst.at[dp], sems.at[0, 0])
    own.start()
    return [own]


def wait_all(copies):
    for copy in copies:
        copy.wait()


def start_reduce(src, got, sems, base, me, n, device):
    copies = []
    for k in range(1, n):
        peer = lax.rem(me + k, n)
        copies.append(send(src.at[peer], got.at[k], sems, base + k, device(peer)))
    return copies


def end_reduce(copies, src, got, me):
    total = src[me].astype(jnp.float32)
    for k, copy in enumerate(copies, 1):
        copy.wait()
        total = total + got[k].astype(jnp.float32)
    return total


def gather_stages(full, sems, base, n_z, n_ten):
    _, z, c, ten = place()
    copies = []
    mine = full.at[c, ten, z]
    for k in range(1, n_z):
        peer = lax.rem(z + k, n_z)
        copies.append(send(mine, mine, sems[0], base * n_z + k, (peer * 2 + c, ten)))
    yield
    wait_all(copies)
    copies = []
    mine = full.at[c, ten]
    for k in range(1, n_ten):
        peer = lax.rem(ten + k, n_ten)
        copies.append(send(mine, mine, sems[1], base * n_ten + k, (z * 2 + c, peer)))
    yield
    wait_all(copies)
    mine = full.at[c]
    copy = send(mine, mine, sems[2], base * 2 + 1, (z * 2 + 1 - c, ten))
    yield
    copy.wait()


def coords_kernel(n_dp, n_ten, g8, part, g_all, full_out, full, got, s_g, s_r, s_z, s_t, s_c):
    n_z = n_dp // 2
    dp, z, c, ten = place()
    near = [k for k in range(1, n_dp) if k < 3 or k > n_dp - 3]
    far = [k for k in range(1, n_dp) if k not in near]
    greet(n_dp, n_ten)
    copies = start_reduce(part, got, s_r, 0, ten, n_ten, lambda p: (dp, p))
    swaps = start_swap(g8, g_all, s_g, n_dp, near) + start_own(g8, g_all, s_g)
    full[c, ten, z] = end_reduce(copies, part, got, ten).astype(full.dtype)
    stages = gather_stages(full, (s_z, s_t, s_c), 0, n_z, n_ten)
    next(stages)
    next(stages)
    if far:
        swaps += start_swap(g8, g_all, s_g, n_dp, far)
    for _ in stages:
        pass
    out = pltpu.make_async_copy(full, full_out, s_c.at[0, 0])
    out.start()
    wait_all(swaps + [out])


def back_kernel(
    n_dp, n_ten, low8, a8, part, low_all, a_all, full_out,
    full, got_c, mid_c, got_t, mid_t, got_z, s_l, s_a, s_rc, s_rt, s_rz, s_z, s_t, s_c,
):
    n_z = n_dp // 2
    dp, z, c, ten = place()
    parts = part.shape[0]

    def stages(p):
        copies = start_reduce(
            part.at[p], got_c.at[p], s_rc, p * 2, c, 2, lambda q: (z * 2 + q, ten)
        )
        yield
        mid_c[p] = end_reduce(copies, part.at[p], got_c.at[p], c).astype(mid_c.dtype)
        copies = start_reduce(
            mid_c.at[p], got_t.at[p], s_rt, p * n_ten, ten, n_ten, lambda q: (dp, q)
        )
        yield
        mid_t[p] = end_reduce(copies, mid_c.at[p], got_t.at[p], ten).astype(mid_t.dtype)
        copies = start_reduce(
            mid_t.at[p], got_z.at[p], s_rz, p * n_z, z, n_z, lambda q: (q * 2 + c, ten)
        )
        yield
        total = end_reduce(copies, mid_t.at[p], got_z.at[p], z)
        full[p, c, ten, z] = total.astype(full.dtype)
        yield from gather_stages(full.at[p], (s_z, s_t, s_c), p, n_z, n_ten)

    greet(n_dp, n_ten)
    chains = [stages(p) for p in range(parts)]
    for chain in chains:
        next(chain)
    swaps = start_swap(low8, low_all, s_l, n_dp) + start_own(low8, low_all, s_l)
    swaps += start_own(a8, a_all, s_a)
    for when in range(1, 6 + parts):
        for p in reversed(range(parts)):
            if 1 <= when - p <= 6:
                next(chains[p], None)
                if p == parts - 1 and when - p == 4:
                    swaps += start_swap(a8, a_all, s_a, n_dp)
    out = pltpu.make_async_copy(full, full_out, s_c.at[0, 0])
    out.start()
    wait_all(swaps + [out])


def swap_kernel(n_dp, src, dst, sems):
    greet(n_dp, 1)
    wait_all(start_swap(src, dst, sems, n_dp) + start_own(src, dst, sems))


def pairs(n):
    return pltpu.SemaphoreType.DMA((2, n))


def params(which):
    return pltpu.CompilerParams(
        collective_id=which, has_side_effects=True, vmem_limit_bytes=32 * 2**20
    )


def like(shape, dtype=jnp.bfloat16):
    return jax.ShapeDtypeStruct(shape, dtype)


def to_blocks(x, n, width):
    rows, cols = x.shape
    x = x.reshape(rows, n, cols // n).transpose(1, 0, 2)
    return jnp.pad(x, ((0, 0), (0, 0), (0, width - cols // n)))


def direct(n_dp, n_ten, acts, grad_out, proj_t, first_moment, second_moment):
    n_z = n_dp // 2
    tok_rows, width = acts.shape
    hidden = grad_out.shape[1]
    rank = proj_t.shape[0]
    rank_rows = first_moment.shape[0]
    tokens = tok_rows * n_dp
    dim = jnp.float32(width * n_ten)
    bf16 = jnp.bfloat16
    h_blk = hidden // n_dp
    h_pad = -(-h_blk // 128) * 128
    w_blk = width // n_dp
    sub = tok_rows // n_ten

    part = (contract_cols(acts, proj_t) * (1.0 / jnp.sqrt(dim))).astype(bf16)
    g8 = to_blocks(grad_out, n_dp, h_pad)
    g_all, coords = pl.pallas_call(
        functools.partial(coords_kernel, n_dp, n_ten),
        out_shape=(like(g8.shape), like((2, n_ten, n_z, sub, rank))),
        in_specs=[ANY, VMEM],
        out_specs=(ANY, ANY),
        scratch_shapes=[
            pltpu.VMEM((2, n_ten, n_z, sub, rank), bf16),
            pltpu.VMEM((n_ten, sub, rank), bf16),
            pairs(n_dp), pairs(n_ten), pairs(n_z), pairs(n_ten), pairs(2),
        ],
        compiler_params=params(0),
    )(g8, part.reshape(n_ten, sub, rank))
    coords = coords.transpose(2, 0, 1, 3, 4).reshape(tokens, rank)
    g_all = g_all.reshape(tokens, h_pad)

    low = (contract_rows(coords, g_all) / tokens).astype(bf16)
    back_part = contract_cols(g_all, low).astype(bf16)
    cross_part = contract_cols(low, low).astype(bf16)
    both = tokens + rank
    blk = both // (n_dp * n_ten)
    joined = jnp.concatenate([back_part, cross_part], axis=0)
    parts = PARTS if blk % (16 * PARTS) == 0 else 1
    joined = joined.reshape(parts, 2, n_ten, n_z, blk // parts, rank)
    a8 = to_blocks(acts, n_dp, w_blk)
    low8 = low.reshape(n_dp, rank_rows, h_pad)
    low_all, a_all, sums = pl.pallas_call(
        functools.partial(back_kernel, n_dp, n_ten),
        out_shape=(like(low8.shape), like(a8.shape), like(joined.shape)),
        in_specs=[ANY, ANY, VMEM],
        out_specs=(ANY, ANY, ANY),
        scratch_shapes=[
            pltpu.VMEM(joined.shape, bf16),
            pltpu.VMEM(joined.shape, bf16),
            pltpu.VMEM((parts,) + joined.shape[2:], bf16),
            pltpu.VMEM((parts,) + joined.shape[2:], bf16),
            pltpu.VMEM((parts,) + joined.shape[3:], bf16),
            pltpu.VMEM((parts,) + joined.shape[3:], bf16),
            pairs(n_dp), pairs(n_dp), pairs(parts * 2), pairs(parts * n_ten), pairs(parts * n_z),
            pairs(parts * n_z), pairs(parts * n_ten), pairs(parts * 2),
        ],
        compiler_params=params(1),
    )(low8, a8, joined)
    sums = sums.reshape(both, rank)
    back_low, cross = sums[:tokens], sums[tokens:]

    dp = lax.axis_index("dp")
    pull = contract_rows(back_low, a_all.reshape(tokens, w_blk)) / tokens
    own_cols = lax.dynamic_slice_in_dim(proj_t, dp * w_blk, w_blk, 1)
    correction = jnp.dot(cross, own_cols, preferred_element_type=jnp.float32)
    delta = (jnp.sqrt(dim) * pull - correction).astype(bf16)
    d8 = delta.reshape(n_dp, rank_rows, w_blk)
    d_all = pl.pallas_call(
        functools.partial(swap_kernel, n_dp),
        out_shape=like(d8.shape),
        in_specs=[ANY],
        out_specs=ANY,
        scratch_shapes=[pairs(n_dp)],
        compiler_params=params(2),
    )(d8)
    own_rows = lax.dynamic_slice_in_dim(proj_t, dp * rank_rows, rank_rows, 0)
    step = d_all.transpose(1, 0, 2).reshape(rank_rows, width)
    new_proj_t = own_rows.astype(jnp.float32) + step.astype(jnp.float32)

    grad_part = low_all[:, :, :h_blk].transpose(1, 0, 2).reshape(rank_rows, hidden)
    return adam(grad_part.astype(jnp.float32), first_moment, second_moment), new_proj_t


def adam(grad_part, first_moment, second_moment):
    moment_one = 0.9 * first_moment + 0.1 * grad_part
    moment_two = 0.999 * second_moment + 0.001 * grad_part * grad_part
    return moment_one / (1.0 - 0.9**10) / (jnp.sqrt(moment_two / (1.0 - 0.999**10)) + 1e-08)


def general(acts, grad_out, proj_t, first_moment, second_moment):
    tok_rows, width = acts.shape
    dim = jnp.float32(width * lax.axis_size("tensor"))
    total_tokens = tok_rows * lax.axis_size("dp")
    rank_rows = first_moment.shape[0]
    row_start = lax.axis_index("dp") * rank_rows
    local_coords = contract_cols(acts, proj_t) * (1.0 / jnp.sqrt(dim))
    coords = lax.psum(local_coords.astype(jnp.bfloat16), "tensor")
    grad_part = lax.psum_scatter(
        contract_rows(coords, grad_out) / total_tokens, "dp", scatter_dimension=0, tiled=True
    )
    low_part = grad_part.astype(jnp.bfloat16)
    piece = lax.all_gather(low_part, "dp", axis=0, tiled=True)
    back = lax.psum(contract_cols(grad_out, piece).astype(jnp.bfloat16), "tensor")
    cross = lax.psum(contract_cols(low_part, piece).astype(jnp.bfloat16), "tensor")
    pull = lax.psum_scatter(
        contract_rows(back, acts) / total_tokens, "dp", scatter_dimension=0, tiled=True
    )
    own_rows = lax.dynamic_slice_in_dim(proj_t, row_start, rank_rows, 0)
    correction = jnp.dot(
        cross.astype(jnp.float32), proj_t.astype(jnp.float32), precision=lax.Precision.HIGHEST
    )
    new_proj_t = own_rows.astype(jnp.float32) + jnp.sqrt(dim) * pull - correction
    return adam(grad_part, first_moment, second_moment), new_proj_t


def local(n_dp, n_ten, acts, grad_out, proj_t, first_moment, second_moment):
    tok_rows, width = acts.shape
    both = tok_rows * n_dp + proj_t.shape[0]
    fits = (
        n_dp % 2 == 0
        and n_dp <= 16
        and tok_rows % (16 * n_ten) == 0
        and both % (16 * n_dp * n_ten) == 0
        and first_moment.shape[0] % 16 == 0
        and width % (128 * n_dp) == 0
        and grad_out.shape[1] % n_dp == 0
    )
    args = (acts, grad_out, proj_t, first_moment, second_moment)
    return direct(n_dp, n_ten, *args) if fits else general(*args)


def solution(mesh):
    split = P("dp", "tensor")
    return jax.shard_map(
        functools.partial(local, mesh.shape["dp"], mesh.shape["tensor"]),
        mesh=mesh,
        in_specs=(split, split, P(None, "tensor"), split, split),
        out_specs=(split, split),
        check_vma=False,
    )
```

```python
import functools

import jax
import jax.numpy as jnp
from jax import lax
from jax.experimental import pallas as pl
from jax.experimental.pallas import tpu as pltpu
from jax.sharding import PartitionSpec as P

MESH = pl.DeviceIdType.MESH
ANY = pl.BlockSpec(memory_space=pl.ANY)
VMEM = pl.BlockSpec(memory_space=pltpu.VMEM)
PARTS = 3


def contract_rows(left, right):
    return lax.dot_general(
        left, right, (((0,), (0,)), ((), ())), preferred_element_type=jnp.float32
    )


def contract_cols(left, right):
    return lax.dot_general(
        left, right, (((1,), (1,)), ((), ())), preferred_element_type=jnp.float32
    )


def place():
    dp = lax.axis_index("dp")
    return dp, lax.div(dp, 2), lax.rem(dp, 2), lax.axis_index("tensor")


def greet(n_dp, n_ten):
    dp, _, _, ten = place()
    barrier = pltpu.get_barrier_semaphore()
    for k in range(1, n_dp):
        pl.semaphore_signal(
            barrier, inc=1, device_id=(lax.rem(dp + k, n_dp), ten), device_id_type=MESH
        )
    for k in range(1, n_ten):
        pl.semaphore_signal(
            barrier, inc=1, device_id=(dp, lax.rem(ten + k, n_ten)), device_id_type=MESH
        )
    pl.semaphore_wait(barrier, n_dp + n_ten - 2)


def send(src, dst, sems, k, device):
    copy = pltpu.make_async_remote_copy(
        src_ref=src,
        dst_ref=dst,
        send_sem=sems.at[0, k],
        recv_sem=sems.at[1, k],
        device_id=device,
        device_id_type=MESH,
    )
    copy.start()
    return copy


def start_swap(src, dst, sems, n_dp, steps=None):
    dp, _, _, ten = place()
    copies = []
    for k in steps or range(1, n_dp):
        peer = lax.rem(dp + k, n_dp)
        copies.append(send(src(peer), dst.at[dp], sems, k, (peer, ten)))
    return copies


def start_own(src, dst, sems):
    dp = place()[0]
    own = pltpu.make_async_copy(src(dp), dst.at[dp], sems.at[0, 0])
    own.start()
    return [own]


def columns(ref, n, span):
    block = ref.shape[1] // n
    return lambda p: ref.at[:, pl.ds(pl.multiple_of(lax.div(p * block, 128) * 128, 128), span)]


def wait_all(copies):
    for copy in copies:
        copy.wait()


def start_reduce(src, got, sems, base, me, n, device):
    copies = []
    for k in range(1, n):
        peer = lax.rem(me + k, n)
        copies.append(send(src.at[peer], got.at[k], sems, base + k, device(peer)))
    return copies


def end_reduce(copies, src, got, me):
    total = src[me].astype(jnp.float32)
    for k, copy in enumerate(copies, 1):
        copy.wait()
        total = total + got[k].astype(jnp.float32)
    return total


def gather_stages(full, sems, base, n_z, n_ten):
    _, z, c, ten = place()
    copies = []
    mine = full.at[c, ten, z]
    for k in range(1, n_z):
        peer = lax.rem(z + k, n_z)
        copies.append(send(mine, mine, sems[0], base * n_z + k, (peer * 2 + c, ten)))
    yield
    wait_all(copies)
    copies = []
    mine = full.at[c, ten]
    for k in range(1, n_ten):
        peer = lax.rem(ten + k, n_ten)
        copies.append(send(mine, mine, sems[1], base * n_ten + k, (z * 2 + c, peer)))
    yield
    wait_all(copies)
    mine = full.at[c]
    copy = send(mine, mine, sems[2], base * 2 + 1, (z * 2 + 1 - c, ten))
    yield
    copy.wait()


def coords_kernel(n_dp, n_ten, grad_out, part, g_all, full_out, full, got, s_g, s_r, s_z, s_t, s_c):
    n_z = n_dp // 2
    dp, z, c, ten = place()
    g8 = columns(grad_out, n_dp, g_all.shape[2])
    near = [k for k in range(1, n_dp) if k < 3 or k > n_dp - 3]
    far = [k for k in range(1, n_dp) if k not in near]
    greet(n_dp, n_ten)
    copies = start_reduce(part, got, s_r, 0, ten, n_ten, lambda p: (dp, p))
    swaps = start_swap(g8, g_all, s_g, n_dp, near) + start_own(g8, g_all, s_g)
    full[c, ten, z] = end_reduce(copies, part, got, ten).astype(full.dtype)
    stages = gather_stages(full, (s_z, s_t, s_c), 0, n_z, n_ten)
    next(stages)
    next(stages)
    if far:
        swaps += start_swap(g8, g_all, s_g, n_dp, far)
    for _ in stages:
        pass
    out = pltpu.make_async_copy(full, full_out, s_c.at[0, 0])
    out.start()
    wait_all(swaps + [out])


def back_kernel(
    n_dp, n_ten, low, acts, part, low_all, a_all, full_out,
    full, got_c, mid_c, got_t, mid_t, got_z, s_l, s_a, s_rc, s_rt, s_rz, s_z, s_t, s_c,
):
    n_z = n_dp // 2
    dp, z, c, ten = place()
    parts = part.shape[0]
    low8 = lambda p: low.at[p]
    a8 = columns(acts, n_dp, a_all.shape[2])

    def stages(p):
        copies = start_reduce(
            part.at[p], got_c.at[p], s_rc, p * 2, c, 2, lambda q: (z * 2 + q, ten)
        )
        yield
        mid_c[p] = end_reduce(copies, part.at[p], got_c.at[p], c).astype(mid_c.dtype)
        copies = start_reduce(
            mid_c.at[p], got_t.at[p], s_rt, p * n_ten, ten, n_ten, lambda q: (dp, q)
        )
        yield
        mid_t[p] = end_reduce(copies, mid_c.at[p], got_t.at[p], ten).astype(mid_t.dtype)
        copies = start_reduce(
            mid_t.at[p], got_z.at[p], s_rz, p * n_z, z, n_z, lambda q: (q * 2 + c, ten)
        )
        yield
        total = end_reduce(copies, mid_t.at[p], got_z.at[p], z)
        full[p, c, ten, z] = total.astype(full.dtype)
        yield from gather_stages(full.at[p], (s_z, s_t, s_c), p, n_z, n_ten)

    greet(n_dp, n_ten)
    chains = [stages(p) for p in range(parts)]
    for chain in chains:
        next(chain)
    swaps = start_swap(low8, low_all, s_l, n_dp) + start_own(low8, low_all, s_l)
    swaps += start_own(a8, a_all, s_a)
    for when in range(1, 6 + parts):
        for p in reversed(range(parts)):
            if 1 <= when - p <= 6:
                next(chains[p], None)
                if p == parts - 1 and when - p == 4:
                    swaps += start_swap(a8, a_all, s_a, n_dp)
    out = pltpu.make_async_copy(full, full_out, s_c.at[0, 0])
    out.start()
    wait_all(swaps + [out])


def finish_kernel(
    n_dp, d8, low_all, first_moment, second_moment, own_rows, adam_step, new_proj_t, got, sems
):
    block = got.shape[2]
    hidden, span = adam_step.shape[1], low_all.shape[2]
    greet(n_dp, 1)
    copies = start_swap(lambda p: d8.at[p], got, sems, n_dp)
    copies += start_own(lambda p: d8.at[p], got, sems)
    for lo in range(0, hidden, 128):
        grad = 0.0
        for p in range(n_dp):
            start, stop = p * hidden // n_dp, (p + 1) * hidden // n_dp
            if start < lo + 128 and stop > lo:
                at = lo - start // 128 * 128
                grad = grad + low_all[p, :, at:at + 128].astype(jnp.float32)
        cols = slice(lo, lo + 128)
        adam_step[:, cols] = adam(grad, first_moment[:, cols], second_moment[:, cols])
    wait_all(copies)
    for p in range(n_dp):
        cols = slice(p * block, (p + 1) * block)
        new_proj_t[:, cols] = own_rows[:, cols].astype(jnp.float32) + got[p].astype(jnp.float32)


def pairs(n):
    return pltpu.SemaphoreType.DMA((2, n))


def params(which):
    return pltpu.CompilerParams(
        collective_id=which, has_side_effects=True, vmem_limit_bytes=32 * 2**20
    )


def like(shape, dtype=jnp.bfloat16):
    return jax.ShapeDtypeStruct(shape, dtype)


def span_of(cols, n):
    block = cols // n
    return max(-(-(p * block % 128 + block) // 128) * 128 for p in range(n))


def direct(n_dp, n_ten, acts, grad_out, proj_t, first_moment, second_moment):
    n_z = n_dp // 2
    tok_rows, width = acts.shape
    hidden = grad_out.shape[1]
    rank = proj_t.shape[0]
    rank_rows = first_moment.shape[0]
    tokens = tok_rows * n_dp
    dim = jnp.float32(width * n_ten)
    bf16 = jnp.bfloat16
    h_blk = hidden // n_dp
    h_pad = span_of(hidden, n_dp)
    w_blk = width // n_dp
    sub = tok_rows // n_ten

    part = (contract_cols(acts, proj_t) * (1.0 / jnp.sqrt(dim))).astype(bf16)
    g_all, coords = pl.pallas_call(
        functools.partial(coords_kernel, n_dp, n_ten),
        out_shape=(like((n_dp, tok_rows, h_pad)), like((2, n_ten, n_z, sub, rank))),
        in_specs=[ANY, VMEM],
        out_specs=(ANY, ANY),
        scratch_shapes=[
            pltpu.VMEM((2, n_ten, n_z, sub, rank), bf16),
            pltpu.VMEM((n_ten, sub, rank), bf16),
            pairs(n_dp), pairs(n_ten), pairs(n_z), pairs(n_ten), pairs(2),
        ],
        compiler_params=params(0),
    )(grad_out, part.reshape(n_ten, sub, rank))
    coords = coords.transpose(2, 0, 1, 3, 4).reshape(tokens, rank)
    g_all = g_all.reshape(tokens, h_pad)

    dp = lax.axis_index("dp")
    place_in = lax.broadcasted_iota(jnp.int32, (1, h_pad), 1) - lax.rem(dp * h_blk, 128)
    low = contract_rows(coords, g_all) / tokens
    low = jnp.where((place_in >= 0) & (place_in < h_blk), low, 0.0).astype(bf16)
    back_part = contract_cols(g_all, low).astype(bf16)
    cross_part = contract_cols(low, low).astype(bf16)
    both = tokens + rank
    blk = both // (n_dp * n_ten)
    joined = jnp.concatenate([back_part, cross_part], axis=0)
    parts = PARTS if blk % (16 * PARTS) == 0 else 1
    joined = joined.reshape(parts, 2, n_ten, n_z, blk // parts, rank)
    low8 = low.reshape(n_dp, rank_rows, h_pad)
    low_all, a_all, sums = pl.pallas_call(
        functools.partial(back_kernel, n_dp, n_ten),
        out_shape=(like(low8.shape), like((n_dp, tok_rows, w_blk)), like(joined.shape)),
        in_specs=[ANY, ANY, VMEM],
        out_specs=(ANY, ANY, ANY),
        scratch_shapes=[
            pltpu.VMEM(joined.shape, bf16),
            pltpu.VMEM(joined.shape, bf16),
            pltpu.VMEM((parts,) + joined.shape[2:], bf16),
            pltpu.VMEM((parts,) + joined.shape[2:], bf16),
            pltpu.VMEM((parts,) + joined.shape[3:], bf16),
            pltpu.VMEM((parts,) + joined.shape[3:], bf16),
            pairs(n_dp), pairs(n_dp), pairs(parts * 2), pairs(parts * n_ten), pairs(parts * n_z),
            pairs(parts * n_z), pairs(parts * n_ten), pairs(parts * 2),
        ],
        compiler_params=params(1),
    )(low8, acts, joined)
    sums = sums.reshape(both, rank)
    back_low, cross = sums[:tokens], sums[tokens:]

    pull = contract_rows(back_low, a_all.reshape(tokens, w_blk)) / tokens
    own_cols = lax.dynamic_slice_in_dim(proj_t, dp * w_blk, w_blk, 1)
    correction = jnp.dot(cross, own_cols, preferred_element_type=jnp.float32)
    delta = (jnp.sqrt(dim) * pull - correction).astype(bf16)
    d8 = delta.reshape(n_dp, rank_rows, w_blk)
    own_rows = lax.dynamic_slice_in_dim(proj_t, dp * rank_rows, rank_rows, 0)
    return pl.pallas_call(
        functools.partial(finish_kernel, n_dp),
        out_shape=(
            like((rank_rows, hidden), jnp.float32), like((rank_rows, width), jnp.float32)
        ),
        in_specs=[ANY, VMEM, VMEM, VMEM, VMEM],
        out_specs=(VMEM, VMEM),
        scratch_shapes=[pltpu.VMEM(d8.shape, bf16), pairs(n_dp)],
        compiler_params=params(2),
    )(d8, low_all, first_moment, second_moment, own_rows)


def adam(grad_part, first_moment, second_moment):
    moment_one = 0.9 * first_moment + 0.1 * grad_part
    moment_two = 0.999 * second_moment + 0.001 * grad_part * grad_part
    return moment_one / (1.0 - 0.9**10) / (jnp.sqrt(moment_two / (1.0 - 0.999**10)) + 1e-08)


def general(acts, grad_out, proj_t, first_moment, second_moment):
    tok_rows, width = acts.shape
    dim = jnp.float32(width * lax.axis_size("tensor"))
    total_tokens = tok_rows * lax.axis_size("dp")
    rank_rows = first_moment.shape[0]
    row_start = lax.axis_index("dp") * rank_rows
    local_coords = contract_cols(acts, proj_t) * (1.0 / jnp.sqrt(dim))
    coords = lax.psum(local_coords.astype(jnp.bfloat16), "tensor")
    grad_part = lax.psum_scatter(
        contract_rows(coords, grad_out) / total_tokens, "dp", scatter_dimension=0, tiled=True
    )
    low_part = grad_part.astype(jnp.bfloat16)
    piece = lax.all_gather(low_part, "dp", axis=0, tiled=True)
    back = lax.psum(contract_cols(grad_out, piece).astype(jnp.bfloat16), "tensor")
    cross = lax.psum(contract_cols(low_part, piece).astype(jnp.bfloat16), "tensor")
    pull = lax.psum_scatter(
        contract_rows(back, acts) / total_tokens, "dp", scatter_dimension=0, tiled=True
    )
    own_rows = lax.dynamic_slice_in_dim(proj_t, row_start, rank_rows, 0)
    correction = jnp.dot(
        cross.astype(jnp.float32), proj_t.astype(jnp.float32), precision=lax.Precision.HIGHEST
    )
    new_proj_t = own_rows.astype(jnp.float32) + jnp.sqrt(dim) * pull - correction
    return adam(grad_part, first_moment, second_moment), new_proj_t


def local(n_dp, n_ten, acts, grad_out, proj_t, first_moment, second_moment):
    tok_rows, width = acts.shape
    both = tok_rows * n_dp + proj_t.shape[0]
    fits = (
        n_dp % 2 == 0
        and n_dp <= 16
        and tok_rows % (16 * n_ten) == 0
        and both % (16 * n_dp * n_ten) == 0
        and first_moment.shape[0] % 16 == 0
        and width % (128 * n_dp) == 0
        and grad_out.shape[1] % (128 * (n_dp // 2)) == 0
    )
    args = (acts, grad_out, proj_t, first_moment, second_moment)
    return direct(n_dp, n_ten, *args) if fits else general(*args)


def solution(mesh):
    split = P("dp", "tensor")
    return jax.shard_map(
        functools.partial(local, mesh.shape["dp"], mesh.shape["tensor"]),
        mesh=mesh,
        in_specs=(split, split, P(None, "tensor"), split, split),
        out_specs=(split, split),
        check_vma=False,
    )
```
